32 devices in a mesh: parts: 2 (over y), node: 4 (over z), local: 4 (over x, core).
Axes of the slice: x: 2, y: 2, z: 4, core: 2. Of those that a mesh axis runs over, the one named last changes fastest.
Arguments:
- hidden_states: bfloat16 [8192, 7168], P(('parts', 'node', 'local')), parts along dimension 0, may hold values from -6 to 6
- expert_ids: int32 [8192, 8], P(('parts', 'node', 'local')), parts along dimension 0, may hold values from 0 to 255, as said below
- route_weights: float32 [8192, 8], P(('parts', 'node', 'local')), parts along dimension 0, may hold values from 0.1 to 0.8
- gate_weight: bfloat16 [4, 7168, 2048], P('local', None, 'node'), may hold values from -0.0625 to 0.0625
- up_weight: bfloat16 [4, 7168, 2048], P('local', None, 'node'), may hold values from -0.0625 to 0.0625
- down_weight: bfloat16 [4, 2048, 7168], P('local', 'node'), may hold values from -0.125 to 0.125
Outputs:
- combined: bfloat16 [8192, 7168], P(('parts', 'node', 'local')), parts along dimension 0
The draws below stay inside these ranges and needn't reach their ends.
There are 2 independent parts, one for each index of `parts`. The reference program is written for one: setup_inputs(seed, part) draws one part's arguments, and reference() takes and returns one part's arrays. A program takes and returns all parts, laid end to end along the dimension named above; an argument that names none is the same for every part. Nothing has to cross between parts.
Inputs may be any that keep to these rules, and one draw needn't show every extreme that they name: `expert_ids`: each token names 8 distinct experts. Of the 256 tokens of one device, at most 5 name any one expert f * 64 (f below 4); in every draw one such expert is named by exactly 5 tokens of every device, and on each device some expert reaches 5.
All inputs are finite; a program needn't handle non-finite values.
Results may differ from the reference program's by a relative error of at most 0.01.
Values may be sent and summed in bfloat16 or wider, within the bound.
A program may use at most 128 MiB of HBM per device.

```python
import jax
import jax.numpy as jnp
from jax import lax

D = 7168
FF = 2048
EXPERTS = 256
TOP = 8
TOK_DEV = 256
CAP = 5
LIVE = 4
TOKENS = 4096
N_NODE = 4


def draw_expert_ids(key, part):
    key = jax.random.fold_in(key, 11)
    blocks = TOKENS // TOK_DEV
    band_width = EXPERTS // TOP
    stride = EXPERTS // LIVE
    subkeys = jax.random.split(key, 7)
    load_count = jax.random.randint(subkeys[0], (blocks, LIVE), 1, CAP + 1)
    favored = jax.random.randint(subkeys[1], (), 0, LIVE)
    busiest = jax.random.randint(subkeys[2], (blocks, 1), 0, LIVE)
    column = jnp.arange(LIVE)[None, :]
    load_count = jnp.where((column == favored) | (column == busiest), CAP, load_count)
    starts = jax.random.randint(subkeys[3], (blocks, LIVE), 0, TOK_DEV)
    places = jax.vmap(lambda subkey: jax.random.permutation(subkey, TOK_DEV))(jax.random.split(subkeys[4], blocks))
    offset = (places[:, :, None] - starts[:, None, :]) % TOK_DEV
    chosen = (offset < load_count[:, None, :]).reshape(TOKENS, LIVE).astype(jnp.int32)
    slot_index = jnp.arange(TOP)
    target = jnp.arange(LIVE) * stride // band_width
    onehot = (target[:, None] == slot_index[None, :]).astype(jnp.int32)
    live_slot = jnp.dot(chosen, onehot)
    filler = jax.random.randint(subkeys[5], (TOKENS, TOP), 1, band_width)
    base_ids = slot_index[None, :] * band_width + jnp.where(live_slot > 0, 0, filler)
    shuffle = jax.vmap(lambda subkey: jax.random.permutation(subkey, TOP))(jax.random.split(subkeys[6], TOKENS))
    return jnp.take_along_axis(base_ids, shuffle, axis=1).astype(jnp.int32)


def levels(rng, dims, cuts, smallest, high):
    def one(axis_at, shards_of):
        draws = jax.random.uniform(jax.random.fold_in(jax.random.fold_in(rng, 6), axis_at), (shards_of,), jnp.float32, smallest / len(cuts), high / len(cuts))
        return jnp.repeat(jnp.exp(draws), dims[axis_at] // shards_of).reshape((-1,) + (1,) * (len(dims) - axis_at - 1))

    level = one(*cuts[0])
    for cut in cuts[1:]:
        level = level * one(*cut)
    return level


def bell_draw(key, shape, width, most, cuts=(), dtype=jnp.bfloat16):
    result = width * jax.random.normal(key, shape, jnp.float32)
    if cuts:
        result = result * levels(key, shape, cuts, -0.22, 0.18)
    return jnp.clip(result, -most, most).astype(dtype)


def setup_inputs(seed: int = 0, part: int = 0) -> dict:
    keys = jax.random.split(jax.random.key(seed), 7)
    part_splits = jax.random.split(jax.random.fold_in(keys[6], part), 7)
    return {
        "hidden_states": bell_draw(part_splits[0], (TOKENS, D), 1.0, 6.0, ((0, 16),)),
        "expert_ids": draw_expert_ids(jax.random.fold_in(jax.random.fold_in(keys[6], part), 71), part),
        "route_weights": jnp.clip(0.1 + 0.7 * jax.random.uniform(part_splits[2], (TOKENS, TOP), jnp.float32) ** levels(part_splits[2], (TOKENS, TOP), ((0, 16),), -0.2, 0.2), 0.1, 0.8),
        "gate_weight": bell_draw(keys[3], (LIVE, D, FF), D ** -0.5, 0.0625, ((0, 4), (2, 4))),
        "up_weight": bell_draw(keys[4], (LIVE, D, FF), D ** -0.5, 0.0625, ((0, 4), (2, 4))),
        "down_weight": bell_draw(keys[5], (LIVE, FF, D), FF ** -0.5, 0.125, ((0, 4), (1, 4))),
    }


def reference(hidden_states, expert_ids, route_weights, gate_weight, up_weight, down_weight):
    stride = EXPERTS // LIVE
    rows_live = (TOKENS // TOK_DEV) * CAP
    slice_width = FF // N_NODE
    combined = jnp.zeros((TOKENS, D), jnp.float32)
    for expert in range(LIVE):
        matched = expert_ids == expert * stride
        weight = jnp.sum(jnp.where(matched, route_weights, jnp.zeros_like(route_weights)), axis=1)
        picked = jnp.any(matched, axis=1)
        row_index = jnp.nonzero(picked, size=rows_live, fill_value=0)[0].astype(jnp.int32)
        is_valid = jnp.arange(rows_live) < jnp.sum(picked.astype(jnp.int32))
        row_block = hidden_states[row_index]
        gate_proj = jnp.dot(row_block, gate_weight[expert], preferred_element_type=jnp.float32)
        up_proj = jnp.dot(row_block, up_weight[expert], preferred_element_type=jnp.float32)
        hidden_act = (jax.nn.silu(gate_proj) * up_proj).astype(jnp.bfloat16)
        partial_sum = jnp.zeros((rows_live, D), jnp.float32)
        for group_index in range(N_NODE):
            first_unit = group_index * slice_width
            slice_term = jnp.dot(hidden_act[:, first_unit:first_unit + slice_width],
                                 down_weight[expert, first_unit:first_unit + slice_width],
                                 preferred_element_type=jnp.float32).astype(jnp.bfloat16)
            slice_term = lax.optimization_barrier(slice_term)
            partial_sum = partial_sum + slice_term.astype(jnp.float32)
        rounded = lax.optimization_barrier(partial_sum.astype(jnp.bfloat16))
        row_scale = jnp.where(is_valid, weight[row_index], jnp.zeros_like(weight[row_index]))
        combined = combined.at[row_index].add(row_scale[:, None].astype(jnp.float32) * rounded.astype(jnp.float32))
    return combined.astype(jnp.bfloat16)
```

```python
import functools

import jax
import jax.numpy as jnp
import numpy as np
from jax import lax
from jax.experimental import pallas as pl
from jax.experimental.pallas import tpu as pltpu
from jax.sharding import PartitionSpec as P

EXPERTS = 256
CAP = 5
TILE = 16
FOLD = TILE // CAP
LANE = 128
PARTS = 4
F32 = jnp.float32
BF16 = jnp.bfloat16
MESH = pl.DeviceIdType.MESH


def plan(width):
    tiles = -(-width // (LANE * FOLD))
    base, extra = divmod(tiles, PARTS)
    chunks, off = [], 0
    for c in range(PARTS):
        w = (base + (c < extra)) * LANE
        chunks.append((off, w))
        off += w
    return tiles * LANE, chunks


def piece(width, strip, chunk, k):
    off, w = chunk
    start = k * strip + off
    return start, min(w, width - start)


def unfold_matrix(group):
    m = np.zeros((FOLD * group * CAP, group * TILE), np.float32)
    for k in range(FOLD):
        for s in range(group):
            for i in range(CAP):
                m[k * group * CAP + s * CAP + i, s * TILE + k * CAP + i] = 1
    return m


def expert_kernel(n_node, n_local, group, strip, chunks, hid, ids, rw, unf, fld, gate, up, down, eo, mix, *scratch):
    nc = len(chunks)
    hid_v, gate_v, up_v, down_v = scratch[:4]
    send_a = scratch[4:4 + nc]
    recv_a = scratch[4 + nc:4 + 2 * nc]
    send_b = scratch[4 + 2 * nc:4 + 3 * nc]
    recv_b = scratch[4 + 3 * nc:4 + 4 * nc]
    hid_sem, wt_sem, sa_sem, ra_sem, sb_sem, rb_sem = scratch[4 + 4 * nc:]
    n = n_node * n_local
    node, local = lax.axis_index("node"), lax.axis_index("local")
    me = node * n_local + local
    tokens, width = hid.shape
    rows = n_local * TILE

    def peer_of(d):
        return lax.rem(me + d, n)

    def at(peer):
        return {"node": peer // n_local, "local": lax.rem(peer, n_local)}

    barrier = pltpu.get_barrier_semaphore()

    @pl.loop(1, n)
    def _(d):
        pl.semaphore_signal(barrier, inc=1, device_id=at(peer_of(d)), device_id_type=MESH)

    hid_copies = []
    for c in range(nc):
        for k in range(FOLD):
            start, w = piece(width, strip, chunks[c], k)
            copy = pltpu.make_async_copy(hid.at[:, pl.ds(start, w)], hid_v.at[:, pl.ds(start, w)], hid_sem.at[c, k])
            copy.start()
            hid_copies.append(copy)
    wt_copies = [
        pltpu.make_async_copy(src.at[0], dst, wt_sem.at[j])
        for j, (src, dst) in enumerate(((gate, gate_v), (up, up_v), (down, down_v)))
    ]
    for copy in wt_copies:
        copy.start()

    row = lax.broadcasted_iota(jnp.int32, (rows, tokens), 0)
    want = (row >> 4) * (EXPERTS // n_local)
    low = row & (TILE - 1)
    strip_of = jnp.zeros_like(low)
    for k in range(1, FOLD + 1):
        strip_of += (low >= k * CAP).astype(jnp.int32)
    slot = low - strip_of * CAP
    match = jnp.zeros((rows, tokens), F32)
    share = jnp.zeros((rows, tokens), F32)
    for j in range(ids.shape[0]):
        hit = ids[j:j + 1, :] == want
        match += jnp.where(hit, 1.0, 0.0)
        share += jnp.where(hit, rw[j:j + 1, :], 0.0)
    before = lax.broadcasted_iota(jnp.int32, (tokens, tokens), 0) < lax.broadcasted_iota(jnp.int32, (tokens, tokens), 1)
    position = jnp.dot(match.astype(BF16), before.astype(F32).astype(BF16), preferred_element_type=F32)
    selected = (match > 0.0) & (position == slot.astype(F32))
    sel = [jnp.where(selected & (strip_of == k), 1.0, 0.0).astype(BF16) for k in range(FOLD)]

    def spread(src, dst, s_sem, r_sem, by_expert):
        @pl.loop(1, n)
        def _(d):
            peer = peer_of(d)
            index = lax.rem(peer, n_local) if by_expert else peer
            pltpu.make_async_remote_copy(
                src_ref=src.at[index],
                dst_ref=dst.at[me],
                send_sem=s_sem,
                recv_sem=r_sem,
                device_id=at(peer),
                device_id_type=MESH,
            ).start()

    def drain(ref, sem):
        others = ref.at[pl.ds(0, n - 1)]
        pltpu.make_async_copy(others, others, sem).wait()

    for c in range(nc):
        w_full = chunks[c][1]
        total = None
        for k in range(FOLD):
            hid_copies[c * FOLD + k].wait()
            start, w = piece(width, strip, chunks[c], k)
            part = jnp.dot(sel[k], hid_v[:, start:start + w], preferred_element_type=F32)
            if w < w_full:
                part = jnp.concatenate([part, jnp.zeros((rows, w_full - w), F32)], axis=1)
            total = part if total is None else total + part
        send_a[c][...] = total.astype(BF16).reshape(n_local, TILE, w_full)
        if c == 0:
            pl.semaphore_wait(barrier, n - 1)
        spread(send_a[c], recv_a[c], sa_sem.at[c], ra_sem.at[c], True)
        recv_a[c][me] = send_a[c][local]

    mixed = jnp.where(selected, share, 0.0)
    for k in range(FOLD):
        m = jnp.where(strip_of == k, mixed, 0.0)
        hi = m.astype(BF16).astype(F32)
        mid = (m - hi).astype(BF16).astype(F32)
        lo = m - hi - mid
        mix[k] = jnp.concatenate([hi, mid, lo], axis=0).T.astype(BF16)

    unfold, fold = unf[...], fld[...]
    per = group * CAP
    gate_sum = up_sum = None
    for c in range(nc):
        w_full = chunks[c][1]
        drain(recv_a[c], ra_sem.at[c])
        if c == 0:
            wt_copies[0].wait()
            wt_copies[1].wait()
        flat = [
            jnp.dot(unfold, recv_a[c][g:g + group].reshape(group * TILE, w_full), preferred_element_type=F32).astype(BF16)
            for g in range(0, n, group)
        ]
        for k in range(FOLD):
            start, w = piece(width, strip, chunks[c], k)
            x = [f[k * per:(k + 1) * per, :w] for f in flat]
            x = x[0] if len(x) == 1 else jnp.concatenate(x, axis=0)
            g = jnp.dot(x, gate_v[start:start + w, :], preferred_element_type=F32)
            u = jnp.dot(x, up_v[start:start + w, :], preferred_element_type=F32)
            gate_sum = g if gate_sum is None else gate_sum + g
            up_sum = u if up_sum is None else up_sum + u
    act = (gate_sum / (1.0 + jnp.exp(-gate_sum)) * up_sum).astype(BF16)

    wt_copies[2].wait()
    for c in range(nc):
        w_full = chunks[c][1]
        y = []
        for k in range(FOLD):
            start, w = piece(width, strip, chunks[c], k)
            part = jnp.dot(act, down_v[:, start:start + w], preferred_element_type=F32).astype(BF16)
            if w < w_full:
                part = jnp.concatenate([part, jnp.zeros((part.shape[0], w_full - w), BF16)], axis=1)
            y.append(part)
        for j, g in enumerate(range(0, n, group)):
            stack = jnp.concatenate([p[j * per:(j + 1) * per] for p in y], axis=0)
            folded = jnp.dot(fold, stack, preferred_element_type=F32).astype(BF16)
            send_b[c][g:g + group] = folded.reshape(group, TILE, w_full)
        spread(send_b[c], recv_b[c], sb_sem.at[c], rb_sem.at[c], False)
        recv_b[c][me] = send_b[c][me]

    for c in range(nc):
        off, w_full = chunks[c]
        drain(recv_b[c], rb_sem.at[c])
        total = recv_b[c][0:n_local].astype(F32)
        for z in range(1, n_node):
            total += recv_b[c][z * n_local:(z + 1) * n_local].astype(F32)
        eo[:, off:off + w_full] = total.astype(BF16).reshape(rows, w_full)
    for c in range(nc):
        drain(recv_a[c], sa_sem.at[c])
        drain(recv_b[c], sb_sem.at[c])


def combine_kernel(strip, chunks, eo, mix, out, buf, sems):
    width = out.shape[1]
    copies = []
    for c, (off, w_full) in enumerate(chunks):
        block = eo[:, off:off + w_full]
        block = jnp.concatenate([block, block, block], axis=0)
        for k in range(FOLD):
            start, w = piece(width, strip, chunks[c], k)
            buf[:, start:start + w] = jnp.dot(mix[k], block[:, :w], preferred_element_type=F32).astype(BF16)
            copy = pltpu.make_async_copy(buf.at[:, pl.ds(start, w)], out.at[:, pl.ds(start, w)], sems.at[c, k])
            copy.start()
            copies.append(copy)
    for copy in copies:
        copy.wait()


def on_device(n_node, n_local, hidden_states, expert_ids, route_weights, gate_weight, up_weight, down_weight):
    tokens, width = hidden_states.shape
    units = gate_weight.shape[2]
    n = n_node * n_local
    group = TILE if n % TILE == 0 else n
    strip, chunks = plan(width)
    nc = len(chunks)
    rows = n_local * TILE
    unf = unfold_matrix(group)
    vmem = pl.BlockSpec(memory_space=pltpu.VMEM)
    hbm = pl.BlockSpec(memory_space=pl.ANY)
    eo, mix = pl.pallas_call(
        functools.partial(expert_kernel, n_node, n_local, group, strip, chunks),
        out_shape=[
            jax.ShapeDtypeStruct((rows, strip), BF16),
            jax.ShapeDtypeStruct((FOLD, tokens, 3 * rows), BF16),
        ],
        in_specs=[hbm, vmem, vmem, vmem, vmem, hbm, hbm, hbm],
        out_specs=[vmem, vmem],
        scratch_shapes=[
            pltpu.VMEM((tokens, width), BF16),
            pltpu.VMEM((width, units), BF16),
            pltpu.VMEM((width, units), BF16),
            pltpu.VMEM((units, width), BF16),
            *[pltpu.VMEM((n_local, TILE, w), BF16) for _, w in chunks],
            *[pltpu.VMEM((n, TILE, w), BF16) for _ in range(3) for _, w in chunks],
            pltpu.SemaphoreType.DMA((nc, FOLD)),
            pltpu.SemaphoreType.DMA((3,)),
            *[pltpu.SemaphoreType.DMA((nc,)) for _ in range(4)],
        ],
        compiler_params=pltpu.CompilerParams(
            collective_id=0, has_side_effects=True, vmem_limit_bytes=60 * 1024 * 1024
        ),
    )(
        hidden_states,
        expert_ids.T,
        route_weights.T,
        jnp.asarray(unf, BF16),
        jnp.asarray(unf.T, BF16),
        gate_weight,
        up_weight,
        down_weight,
    )
    return pl.pallas_call(
        functools.partial(combine_kernel, strip, chunks),
        out_shape=jax.ShapeDtypeStruct((tokens, width), BF16),
        in_specs=[vmem, vmem],
        out_specs=hbm,
        scratch_shapes=[pltpu.VMEM((tokens, width), BF16), pltpu.SemaphoreType.DMA((nc, FOLD))],
        compiler_params=pltpu.CompilerParams(vmem_limit_bytes=32 * 1024 * 1024),
    )(eo, mix)


def solution(mesh):
    placed = (
        P(("parts", "node", "local"), None),
        P(("parts", "node", "local"), None),
        P(("parts", "node", "local"), None),
        P("local", None, "node"),
        P("local", None, "node"),
        P("local", "node", None),
    )
    return jax.shard_map(
        functools.partial(on_device, mesh.shape["node"], mesh.shape["local"]),
        mesh=mesh,
        in_specs=placed,
        out_specs=P(("parts", "node", "local"), None),
        check_vma=False,
    )
```

```python
import functools

import jax
import jax.numpy as jnp
import numpy as np
from jax import lax
from jax.experimental import pallas as pl
from jax.experimental.pallas import tpu as pltpu
from jax.sharding import PartitionSpec as P

EXPERTS = 256
CAP = 5
TILE = 16
FOLD = TILE // CAP
LANE = 128
PARTS = 4
F32 = jnp.float32
BF16 = jnp.bfloat16
MESH = pl.DeviceIdType.MESH


def plan(width):
    tiles = -(-width // (LANE * FOLD))
    base, extra = divmod(tiles, PARTS)
    chunks, off = [], 0
    for c in range(PARTS):
        w = (base + (c < extra)) * LANE
        chunks.append((off, w))
        off += w
    return tiles * LANE, chunks


def piece(width, strip, chunk, k):
    off, w = chunk
    start = k * strip + off
    return start, min(w, width - start)


def unfold_matrix(group):
    m = np.zeros((FOLD * group * CAP, group * TILE), np.float32)
    for k in range(FOLD):
        for s in range(group):
            for i in range(CAP):
                m[k * group * CAP + s * CAP + i, s * TILE + k * CAP + i] = 1
    return m


def expert_kernel(n_node, n_local, group, strip, chunks, hid, ids, rw, unf, fld, gate, up, down, eo, mix, *scratch):
    nc = len(chunks)
    hid_v, gate_v, up_v, down_v = scratch[:4]
    send_a = scratch[4:4 + nc]
    recv_a = scratch[4 + nc:4 + 2 * nc]
    send_b = scratch[4 + 2 * nc:4 + 3 * nc]
    recv_b = scratch[4 + 3 * nc:4 + 4 * nc]
    back = scratch[4 + 4 * nc:4 + 5 * nc]
    (hid_sem, wt_sem, loc_send, loc_recv, in_send, in_recv, out_send, out_recv, back_send, back_recv) = scratch[4 + 5 * nc:]
    n = n_node * n_local
    node, local = lax.axis_index("node"), lax.axis_index("local")
    tokens, width = hid.shape
    rows = n_local * TILE
    has_left, has_right = node > 0, node < n_node - 1
    is_first, is_last = node == 0, node == n_node - 1
    left, right = {"node": node - 1}, {"node": node + 1}

    def plane(ref, s):
        return ref.at[pl.ds(s * n_local, n_local)]

    def greet(where):
        pl.semaphore_signal(barrier, inc=1, device_id=where, device_id_type=MESH)

    barrier = pltpu.get_barrier_semaphore()

    @pl.loop(1, n_local)
    def _(d):
        greet({"local": lax.rem(local + d, n_local)})

    @pl.when(has_left)
    def _():
        greet(left)

    @pl.when(has_right)
    def _():
        greet(right)

    hid_copies = []
    for c in range(nc):
        for k in range(FOLD):
            start, w = piece(width, strip, chunks[c], k)
            copy = pltpu.make_async_copy(hid.at[:, pl.ds(start, w)], hid_v.at[:, pl.ds(start, w)], hid_sem.at[c, k])
            copy.start()
            hid_copies.append(copy)
    wt_copies = [
        pltpu.make_async_copy(src.at[0], dst, wt_sem.at[j])
        for j, (src, dst) in enumerate(((gate, gate_v), (up, up_v), (down, down_v)))
    ]
    for copy in wt_copies:
        copy.start()

    row = lax.broadcasted_iota(jnp.int32, (rows, tokens), 0)
    want = (row >> 4) * (EXPERTS // n_local)
    low = row & (TILE - 1)
    strip_of = jnp.zeros_like(low)
    for k in range(1, FOLD + 1):
        strip_of += (low >= k * CAP).astype(jnp.int32)
    slot = low - strip_of * CAP
    match = jnp.zeros((rows, tokens), F32)
    share = jnp.zeros((rows, tokens), F32)
    for j in range(ids.shape[0]):
        hit = ids[j:j + 1, :] == want
        match += jnp.where(hit, 1.0, 0.0)
        share += jnp.where(hit, rw[j:j + 1, :], 0.0)
    before = lax.broadcasted_iota(jnp.int32, (tokens, tokens), 0) < lax.broadcasted_iota(jnp.int32, (tokens, tokens), 1)
    position = jnp.dot(match.astype(BF16), before.astype(F32).astype(BF16), preferred_element_type=F32)
    selected = (match > 0.0) & (position == slot.astype(F32))
    sel = [jnp.where(selected & (strip_of == k), 1.0, 0.0).astype(BF16) for k in range(FOLD)]

    def to_locals(src, base, dst, index, s_sem, r_sem):
        @pl.loop(1, n_local)
        def _(d):
            peer = lax.rem(local + d, n_local)
            pltpu.make_async_remote_copy(
                src_ref=src.at[base + peer],
                dst_ref=dst.at[index],
                send_sem=s_sem,
                recv_sem=r_sem,
                device_id={"local": peer},
                device_id_type=MESH,
            ).start()

    def drain_locals(ref, sem):
        others = ref.at[pl.ds(0, n_local - 1)]
        pltpu.make_async_copy(others, others, sem).wait()

    def in_copy(c, s, where, way):
        return pltpu.make_async_remote_copy(
            src_ref=plane(recv_a[c], s),
            dst_ref=plane(recv_a[c], s),
            send_sem=in_send.at[c, s, way],
            recv_sem=in_recv.at[c, s],
            device_id=where,
            device_id_type=MESH,
        )

    def out_copy(c, s, place, where):
        return pltpu.make_async_remote_copy(
            src_ref=plane(send_b[c], s),
            dst_ref=plane(recv_b[c], place),
            send_sem=out_send.at[c, s],
            recv_sem=out_recv.at[c, place],
            device_id=where,
            device_id_type=MESH,
        )

    def arrived(ref, sem):
        pltpu.make_async_copy(ref, ref, sem).wait()

    for c in range(nc):
        w_full = chunks[c][1]
        total = None
        for k in range(FOLD):
            hid_copies[c * FOLD + k].wait()
            start, w = piece(width, strip, chunks[c], k)
            part = jnp.dot(sel[k], hid_v[:, start:start + w], preferred_element_type=F32)
            if w < w_full:
                part = jnp.concatenate([part, jnp.zeros((rows, w_full - w), F32)], axis=1)
            total = part if total is None else total + part
        send_a[c][...] = total.astype(BF16).reshape(n_local, TILE, w_full)
        if c == 0:
            pl.semaphore_wait(barrier, n_local - 1 + has_left.astype(jnp.int32) + has_right.astype(jnp.int32))
        to_locals(send_a[c], 0, recv_a[c], node * n_local + local, loc_send.at[c], loc_recv.at[c])
        recv_a[c][node * n_local + local] = send_a[c][local]

    for c in range(nc):
        drain_locals(send_a[c], loc_recv.at[c])

        @pl.when(has_right)
        def _():
            in_copy(c, node, right, 0).start()

        @pl.when(has_left)
        def _():
            in_copy(c, node, left, 1).start()

    mixed = jnp.where(selected, share, 0.0)
    for k in range(FOLD):
        m = jnp.where(strip_of == k, mixed, 0.0)
        hi = m.astype(BF16).astype(F32)
        mid = (m - hi).astype(BF16).astype(F32)
        lo = m - hi - mid
        mix[k] = jnp.concatenate([hi, mid, lo], axis=0).T.astype(BF16)

    for c in range(nc):
        @pl.when(is_first)
        def _():
            recv_b[c][0:n_local] = jnp.zeros((n_local, TILE, chunks[c][1]), BF16)

        @pl.when(is_last)
        def _():
            recv_b[c][n:n + n_local] = jnp.zeros((n_local, TILE, chunks[c][1]), BF16)

    @pl.loop(1, n_node)
    def _(h):
        for c in range(nc):
            @pl.when((node - h >= 0) & has_right)
            def _():
                arrived(plane(recv_a[c], node - h), in_recv.at[c, node - h])
                in_copy(c, node - h, right, 0).start()

            @pl.when((node + h < n_node) & has_left)
            def _():
                arrived(plane(recv_a[c], node + h), in_recv.at[c, node + h])
                in_copy(c, node + h, left, 1).start()

    unfold, fold = unf[...], fld[...]
    per = group * CAP
    gate_sum = up_sum = None
    for c in range(nc):
        w_full = chunks[c][1]

        @pl.when(is_last)
        def _():
            @pl.loop(0, n_node - 1)
            def _(s):
                arrived(plane(recv_a[c], s), in_recv.at[c, s])

        @pl.when(is_first)
        def _():
            @pl.loop(1, n_node)
            def _(s):
                arrived(plane(recv_a[c], s), in_recv.at[c, s])

        if c == 0:
            wt_copies[0].wait()
            wt_copies[1].wait()
        flat = [
            jnp.dot(unfold, recv_a[c][g:g + group].reshape(group * TILE, w_full), preferred_element_type=F32).astype(BF16)
            for g in range(0, n, group)
        ]
        for k in range(FOLD):
            start, w = piece(width, strip, chunks[c], k)
            x = [f[k * per:(k + 1) * per, :w] for f in flat]
            x = x[0] if len(x) == 1 else jnp.concatenate(x, axis=0)
            g = jnp.dot(x, gate_v[start:start + w, :], preferred_element_type=F32)
            u = jnp.dot(x, up_v[start:start + w, :], preferred_element_type=F32)
            gate_sum = g if gate_sum is None else gate_sum + g
            up_sum = u if up_sum is None else up_sum + u
    act = (gate_sum / (1.0 + jnp.exp(-gate_sum)) * up_sum).astype(BF16)

    wt_copies[2].wait()

    def partial_sums(c):
        w_full = chunks[c][1]
        y = []
        for k in range(FOLD):
            start, w = piece(width, strip, chunks[c], k)
            part = jnp.dot(act, down_v[:, start:start + w], preferred_element_type=F32).astype(BF16)
            if w < w_full:
                part = jnp.concatenate([part, jnp.zeros((part.shape[0], w_full - w), BF16)], axis=1)
            y.append(part)
        for j, g in enumerate(range(0, n, group)):
            stack = jnp.concatenate([p[j * per:(j + 1) * per] for p in y], axis=0)
            folded = jnp.dot(fold, stack, preferred_element_type=F32).astype(BF16)
            send_b[c][g:g + group] = folded.reshape(group, TILE, w_full)

    def add(c, s):
        there = pl.ds(s * n_local, n_local)
        send_b[c][there] = (send_b[c][there].astype(F32) + recv_b[c][there].astype(F32)).astype(BF16)

    for c in range(nc):
        partial_sums(c)

        @pl.when(is_first)
        def _():
            out_copy(c, n_node - 1, n_node - 1, right).start()

        @pl.when(is_last)
        def _():
            out_copy(c, 0, lax.select(node == 1, n_node, 0), left).start()

    @pl.loop(0, n_node - 1)
    def _(e):
        h = n_node - 1 - e
        for c in range(nc):
            @pl.when((node + h < n_node) & (h < n_node - 1))
            def _():
                @pl.when(has_left)
                def _():
                    arrived(plane(recv_b[c], node + h), out_recv.at[c, node + h])
                    add(c, node + h)

                out_copy(c, node + h, node + h, right).start()

            @pl.when((node - h >= 0) & (h < n_node - 1))
            def _():
                @pl.when(has_right)
                def _():
                    arrived(plane(recv_b[c], node - h), out_recv.at[c, node - h])
                    add(c, node - h)

                out_copy(c, node - h, lax.select(h == 1, n_node, node - h), left).start()

    for c in range(nc):
        @pl.when(has_left)
        def _():
            arrived(plane(recv_b[c], node), out_recv.at[c, node])

        @pl.when(has_right)
        def _():
            arrived(plane(recv_b[c], n_node), out_recv.at[c, n_node])

        here = pl.ds(node * n_local, n_local)
        total = send_b[c][here].astype(F32) + recv_b[c][here].astype(F32) + recv_b[c][n:n + n_local].astype(F32)
        send_b[c][here] = total.astype(BF16)
        to_locals(send_b[c], node * n_local, back[c], local, back_send.at[c], back_recv.at[c])
        back[c][local] = send_b[c][node * n_local + local]

    for c in range(nc):
        off, w_full = chunks[c]
        drain_locals(send_a[c], back_recv.at[c])
        eo[:, off:off + w_full] = back[c][...].reshape(rows, w_full)

    for c in range(nc):
        drain_locals(send_a[c], loc_send.at[c])
        drain_locals(send_a[c], back_send.at[c])

        @pl.loop(0, n_node)
        def _(s):
            @pl.when((s <= node) & has_right)
            def _():
                arrived(plane(recv_a[c], s), in_send.at[c, s, 0])

            @pl.when((s >= node) & has_left)
            def _():
                arrived(plane(recv_a[c], s), in_send.at[c, s, 1])

            @pl.when(s != node)
            def _():
                arrived(plane(send_b[c], s), out_send.at[c, s])


def combine_kernel(strip, chunks, eo, mix, out, buf, sems):
    width = out.shape[1]
    copies = []
    for c, (off, w_full) in enumerate(chunks):
        block = eo[:, off:off + w_full]
        block = jnp.concatenate([block, block, block], axis=0)
        for k in range(FOLD):
            start, w = piece(width, strip, chunks[c], k)
            buf[:, start:start + w] = jnp.dot(mix[k], block[:, :w], preferred_element_type=F32).astype(BF16)
            copy = pltpu.make_async_copy(buf.at[:, pl.ds(start, w)], out.at[:, pl.ds(start, w)], sems.at[c, k])
            copy.start()
            copies.append(copy)
    for copy in copies:
        copy.wait()


def on_device(n_node, n_local, hidden_states, expert_ids, route_weights, gate_weight, up_weight, down_weight):
    tokens, width = hidden_states.shape
    units = gate_weight.shape[2]
    n = n_node * n_local
    group = TILE if n % TILE == 0 else n
    strip, chunks = plan(width)
    nc = len(chunks)
    rows = n_local * TILE
    unf = unfold_matrix(group)
    vmem = pl.BlockSpec(memory_space=pltpu.VMEM)
    hbm = pl.BlockSpec(memory_space=pl.ANY)
    eo, mix = pl.pallas_call(
        functools.partial(expert_kernel, n_node, n_local, group, strip, chunks),
        out_shape=[
            jax.ShapeDtypeStruct((rows, strip), BF16),
            jax.ShapeDtypeStruct((FOLD, tokens, 3 * rows), BF16),
        ],
        in_specs=[hbm, vmem, vmem, vmem, vmem, hbm, hbm, hbm],
        out_specs=[vmem, vmem],
        scratch_shapes=[
            pltpu.VMEM((tokens, width), BF16),
            pltpu.VMEM((width, units), BF16),
            pltpu.VMEM((width, units), BF16),
            pltpu.VMEM((units, width), BF16),
            *[pltpu.VMEM((n_local, TILE, w), BF16) for _, w in chunks],
            *[pltpu.VMEM((n, TILE, w), BF16) for _ in range(2) for _, w in chunks],
            *[pltpu.VMEM((n + n_local, TILE, w), BF16) for _, w in chunks],
            *[pltpu.VMEM((n_local, TILE, w), BF16) for _, w in chunks],
            pltpu.SemaphoreType.DMA((nc, FOLD)),
            pltpu.SemaphoreType.DMA((3,)),
            pltpu.SemaphoreType.DMA((nc,)),
            pltpu.SemaphoreType.DMA((nc,)),
            pltpu.SemaphoreType.DMA((nc, n_node, 2)),
            pltpu.SemaphoreType.DMA((nc, n_node)),
            pltpu.SemaphoreType.DMA((nc, n_node)),
            pltpu.SemaphoreType.DMA((nc, n_node + 1)),
            pltpu.SemaphoreType.DMA((nc,)),
            pltpu.SemaphoreType.DMA((nc,)),
        ],
        compiler_params=pltpu.CompilerParams(
            collective_id=0, has_side_effects=True, vmem_limit_bytes=60 * 1024 * 1024
        ),
    )(
        hidden_states,
        expert_ids.T,
        route_weights.T,
        jnp.asarray(unf, BF16),
        jnp.asarray(unf.T, BF16),
        gate_weight,
        up_weight,
        down_weight,
    )
    return pl.pallas_call(
        functools.partial(combine_kernel, strip, chunks),
        out_shape=jax.ShapeDtypeStruct((tokens, width), BF16),
        in_specs=[vmem, vmem],
        out_specs=hbm,
        scratch_shapes=[pltpu.VMEM((tokens, width), BF16), pltpu.SemaphoreType.DMA((nc, FOLD))],
        compiler_params=pltpu.CompilerParams(vmem_limit_bytes=32 * 1024 * 1024),
    )(eo, mix)


def solution(mesh):
    placed = (
        P(("parts", "node", "local"), None),
        P(("parts", "node", "local"), None),
        P(("parts", "node", "local"), None),
        P("local", None, "node"),
        P("local", None, "node"),
        P("local", "node", None),
    )
    return jax.shard_map(
        functools.partial(on_device, mesh.shape["node"], mesh.shape["local"]),
        mesh=mesh,
        in_specs=placed,
        out_specs=P(("parts", "node", "local"), None),
        check_vma=False,
    )
```

```python
import functools

import jax
import jax.numpy as jnp
import numpy as np
from jax import lax
from jax.experimental import pallas as pl
from jax.experimental.pallas import tpu as pltpu
from jax.sharding import PartitionSpec as P

EXPERTS = 256
CAP = 5
TILE = 16
FOLD = TILE // CAP
LANE = 128
PARTS = 4
F32 = jnp.float32
BF16 = jnp.bfloat16
MESH = pl.DeviceIdType.MESH


def plan(width):
    tiles = -(-width // (LANE * FOLD))
    base, extra = divmod(tiles, PARTS)
    chunks, off = [], 0
    for c in range(PARTS):
        w = (base + (c < extra)) * LANE
        chunks.append((off, w))
        off += w
    return tiles * LANE, chunks


def piece(width, strip, chunk, k):
    off, w = chunk
    start = k * strip + off
    return start, min(w, width - start)


def unfold_matrix(group):
    m = np.zeros((FOLD * group * CAP, group * TILE), np.float32)
    for k in range(FOLD):
        for s in range(group):
            for i in range(CAP):
                m[k * group * CAP + s * CAP + i, s * TILE + k * CAP + i] = 1
    return m


def expert_kernel(n_node, n_local, group, strip, chunks, hid, ids, rw, unf, fld, gate, up, down, eo, mix, *scratch):
    nc = len(chunks)
    hid_v, gate_v, up_v, down_v = scratch[:4]
    send_a = scratch[4:4 + nc]
    recv_a = scratch[4 + nc:4 + 2 * nc]
    send_b = scratch[4 + 2 * nc:4 + 3 * nc]
    recv_b = scratch[4 + 3 * nc:4 + 4 * nc]
    back = scratch[4 + 4 * nc:4 + 5 * nc]
    (hid_sem, wt_sem, loc_send, loc_recv, in_send, in_recv, out_send, out_recv, back_send, back_recv) = scratch[4 + 5 * nc:]
    n = n_node * n_local
    node, local = lax.axis_index("node"), lax.axis_index("local")
    tokens, width = hid.shape
    rows = n_local * TILE
    has_left, has_right = node > 0, node < n_node - 1
    is_first, is_last = node == 0, node == n_node - 1
    left, right = {"node": node - 1}, {"node": node + 1}

    def plane(ref, s):
        return ref.at[pl.ds(s * n_local, n_local)]

    def greet(where):
        pl.semaphore_signal(barrier, inc=1, device_id=where, device_id_type=MESH)

    barrier = pltpu.get_barrier_semaphore()

    @pl.loop(1, n_local)
    def _(d):
        greet({"local": lax.rem(local + d, n_local)})

    @pl.when(has_left)
    def _():
        greet(left)

    @pl.when(has_right)
    def _():
        greet(right)

    hid_copies = []
    for c in range(nc):
        for k in range(FOLD):
            start, w = piece(width, strip, chunks[c], k)
            copy = pltpu.make_async_copy(hid.at[:, pl.ds(start, w)], hid_v.at[:, pl.ds(start, w)], hid_sem.at[c, k])
            copy.start()
            hid_copies.append(copy)
    wt_copies = [
        pltpu.make_async_copy(src.at[0], dst, wt_sem.at[j])
        for j, (src, dst) in enumerate(((gate, gate_v), (up, up_v), (down, down_v)))
    ]

    row = lax.broadcasted_iota(jnp.int32, (rows, tokens), 0)
    want = (row >> 4) * (EXPERTS // n_local)
    low = row & (TILE - 1)
    strip_of = jnp.zeros_like(low)
    for k in range(1, FOLD + 1):
        strip_of += (low >= k * CAP).astype(jnp.int32)
    slot = low - strip_of * CAP
    match = jnp.zeros((rows, tokens), F32)
    share = jnp.zeros((rows, tokens), F32)
    for j in range(ids.shape[0]):
        hit = ids[j:j + 1, :] == want
        match += jnp.where(hit, 1.0, 0.0)
        share += jnp.where(hit, rw[j:j + 1, :], 0.0)
    before = lax.broadcasted_iota(jnp.int32, (tokens, tokens), 0) < lax.broadcasted_iota(jnp.int32, (tokens, tokens), 1)
    position = jnp.dot(match.astype(BF16), before.astype(F32).astype(BF16), preferred_element_type=F32)
    selected = (match > 0.0) & (position == slot.astype(F32))
    sel = [jnp.where(selected & (strip_of == k), 1.0, 0.0).astype(BF16) for k in range(FOLD)]

    def to_locals(src, base, dst, index, s_sem, r_sem):
        @pl.loop(1, n_local)
        def _(d):
            peer = lax.rem(local + d, n_local)
            pltpu.make_async_remote_copy(
                src_ref=src.at[base + peer],
                dst_ref=dst.at[index],
                send_sem=s_sem,
                recv_sem=r_sem,
                device_id={"local": peer},
                device_id_type=MESH,
            ).start()

    def drain_locals(ref, sem):
        others = ref.at[pl.ds(0, n_local - 1)]
        pltpu.make_async_copy(others, others, sem).wait()

    def in_copy(c, s, where, way):
        return pltpu.make_async_remote_copy(
            src_ref=plane(recv_a[c], s),
            dst_ref=plane(recv_a[c], s),
            send_sem=in_send.at[c, s, way],
            recv_sem=in_recv.at[c, s],
            device_id=where,
            device_id_type=MESH,
        )

    def out_copy(c, s, place, where):
        return pltpu.make_async_remote_copy(
            src_ref=plane(send_b[c], s),
            dst_ref=plane(recv_b[c], place),
            send_sem=out_send.at[c, s],
            recv_sem=out_recv.at[c, place],
            device_id=where,
            device_id_type=MESH,
        )

    def arrived(ref, sem):
        pltpu.make_async_copy(ref, ref, sem).wait()

    for c in range(nc):
        w_full = chunks[c][1]
        total = None
        for k in range(FOLD):
            hid_copies[c * FOLD + k].wait()
            start, w = piece(width, strip, chunks[c], k)
            part = jnp.dot(sel[k], hid_v[:, start:start + w], preferred_element_type=F32)
            if w < w_full:
                part = jnp.concatenate([part, jnp.zeros((rows, w_full - w), F32)], axis=1)
            total = part if total is None else total + part
        send_a[c][...] = total.astype(BF16).reshape(n_local, TILE, w_full)
        if c == 0:
            pl.semaphore_wait(barrier, n_local - 1 + has_left.astype(jnp.int32) + has_right.astype(jnp.int32))
        to_locals(send_a[c], 0, recv_a[c], node * n_local + local, loc_send.at[c], loc_recv.at[c])
        recv_a[c][node * n_local + local] = send_a[c][local]

    for c in range(nc):
        drain_locals(send_a[c], loc_recv.at[c])

        @pl.when(has_right)
        def _():
            in_copy(c, node, right, 0).start()

        @pl.when(has_left)
        def _():
            in_copy(c, node, left, 1).start()

    for copy in wt_copies:
        copy.start()

    mixed = jnp.where(selected, share, 0.0)
    for k in range(FOLD):
        m = jnp.where(strip_of == k, mixed, 0.0)
        hi = m.astype(BF16).astype(F32)
        mid = (m - hi).astype(BF16).astype(F32)
        lo = m - hi - mid
        mix[k] = jnp.concatenate([hi, mid, lo], axis=0).T.astype(BF16)

    for c in range(nc):
        @pl.when(is_first)
        def _():
            recv_b[c][0:n_local] = jnp.zeros((n_local, TILE, chunks[c][1]), BF16)

        @pl.when(is_last)
        def _():
            recv_b[c][n:n + n_local] = jnp.zeros((n_local, TILE, chunks[c][1]), BF16)

    @pl.loop(1, n_node)
    def _(h):
        for c in range(nc):
            @pl.when((node - h >= 0) & has_right)
            def _():
                arrived(plane(recv_a[c], node - h), in_recv.at[c, node - h])
                in_copy(c, node - h, right, 0).start()

            @pl.when((node + h < n_node) & has_left)
            def _():
                arrived(plane(recv_a[c], node + h), in_recv.at[c, node + h])
                in_copy(c, node + h, left, 1).start()

    unfold, fold = unf[...], fld[...]
    per = group * CAP
    gate_sum = up_sum = None
    for c in range(nc):
        w_full = chunks[c][1]

        @pl.when(is_last)
        def _():
            @pl.loop(0, n_node - 1)
            def _(s):
                arrived(plane(recv_a[c], s), in_recv.at[c, s])

        @pl.when(is_first)
        def _():
            @pl.loop(1, n_node)
            def _(s):
                arrived(plane(recv_a[c], s), in_recv.at[c, s])

        if c == 0:
            wt_copies[0].wait()
            wt_copies[1].wait()
        flat = [
            jnp.dot(unfold, recv_a[c][g:g + group].reshape(group * TILE, w_full), preferred_element_type=F32).astype(BF16)
            for g in range(0, n, group)
        ]
        for k in range(FOLD):
            start, w = piece(width, strip, chunks[c], k)
            x = [f[k * per:(k + 1) * per, :w] for f in flat]
            x = x[0] if len(x) == 1 else jnp.concatenate(x, axis=0)
            g = jnp.dot(x, gate_v[start:start + w, :], preferred_element_type=F32)
            u = jnp.dot(x, up_v[start:start + w, :], preferred_element_type=F32)
            gate_sum = g if gate_sum is None else gate_sum + g
            up_sum = u if up_sum is None else up_sum + u
    act = (gate_sum / (1.0 + jnp.exp(-gate_sum)) * up_sum).astype(BF16)

    wt_copies[2].wait()

    def partial_sums(c):
        w_full = chunks[c][1]
        y = []
        for k in range(FOLD):
            start, w = piece(width, strip, chunks[c], k)
            part = jnp.dot(act, down_v[:, start:start + w], preferred_element_type=F32).astype(BF16)
            if w < w_full:
                part = jnp.concatenate([part, jnp.zeros((part.shape[0], w_full - w), BF16)], axis=1)
            y.append(part)
        for j, g in enumerate(range(0, n, group)):
            stack = jnp.concatenate([p[j * per:(j + 1) * per] for p in y], axis=0)
            folded = jnp.dot(fold, stack, preferred_element_type=F32).astype(BF16)
            send_b[c][g:g + group] = folded.reshape(group, TILE, w_full)

    def add(c, s):
        there = pl.ds(s * n_local, n_local)
        send_b[c][there] = (send_b[c][there].astype(F32) + recv_b[c][there].astype(F32)).astype(BF16)

    for c in range(nc):
        partial_sums(c)

        @pl.when(is_first)
        def _():
            out_copy(c, n_node - 1, n_node - 1, right).start()

        @pl.when(is_last)
        def _():
            out_copy(c, 0, lax.select(node == 1, n_node, 0), left).start()

    @pl.loop(0, n_node - 1)
    def _(e):
        h = n_node - 1 - e
        for c in range(nc):
            @pl.when((node + h < n_node) & (h < n_node - 1))
            def _():
                @pl.when(has_left)
                def _():
                    arrived(plane(recv_b[c], node + h), out_recv.at[c, node + h])
                    add(c, node + h)

                out_copy(c, node + h, node + h, right).start()

            @pl.when((node - h >= 0) & (h < n_node - 1))
            def _():
                @pl.when(has_right)
                def _():
                    arrived(plane(recv_b[c], node - h), out_recv.at[c, node - h])
                    add(c, node - h)

                out_copy(c, node - h, lax.select(h == 1, n_node, node - h), left).start()

    for c in range(nc):
        @pl.when(has_left)
        def _():
            arrived(plane(recv_b[c], node), out_recv.at[c, node])

        @pl.when(has_right)
        def _():
            arrived(plane(recv_b[c], n_node), out_recv.at[c, n_node])

        here = pl.ds(node * n_local, n_local)
        total = send_b[c][here].astype(F32) + recv_b[c][here].astype(F32) + recv_b[c][n:n + n_local].astype(F32)
        send_b[c][here] = total.astype(BF16)
        to_locals(send_b[c], node * n_local, back[c], local, back_send.at[c], back_recv.at[c])
        back[c][local] = send_b[c][node * n_local + local]

    for c in range(nc):
        off, w_full = chunks[c]
        drain_locals(send_a[c], back_recv.at[c])
        eo[:, off:off + w_full] = back[c][...].reshape(rows, w_full)

    for c in range(nc):
        drain_locals(send_a[c], loc_send.at[c])
        drain_locals(send_a[c], back_send.at[c])

        @pl.loop(0, n_node)
        def _(s):
            @pl.when((s <= node) & has_right)
            def _():
                arrived(plane(recv_a[c], s), in_send.at[c, s, 0])

            @pl.when((s >= node) & has_left)
            def _():
                arrived(plane(recv_a[c], s), in_send.at[c, s, 1])

            @pl.when(s != node)
            def _():
                arrived(plane(send_b[c], s), out_send.at[c, s])


def combine_kernel(strip, chunks, eo_hbm, mix_hbm, out, eo, mix, buf, in_sems, sems):
    width = out.shape[1]
    loads = [
        pltpu.make_async_copy(src, dst, in_sems.at[j])
        for j, (src, dst) in enumerate(((eo_hbm, eo), (mix_hbm, mix)))
    ]
    for copy in loads:
        copy.start()
    for copy in loads:
        copy.wait()
    copies = []
    for c, (off, w_full) in enumerate(chunks):
        block = eo[:, off:off + w_full]
        block = jnp.concatenate([block, block, block], axis=0)
        for k in range(FOLD):
            start, w = piece(width, strip, chunks[c], k)
            buf[:, start:start + w] = jnp.dot(mix[k], block[:, :w], preferred_element_type=F32).astype(BF16)
            copy = pltpu.make_async_copy(buf.at[:, pl.ds(start, w)], out.at[:, pl.ds(start, w)], sems.at[c, k])
            copy.start()
            copies.append(copy)
    for copy in copies:
        copy.wait()


def on_device(n_node, n_local, hidden_states, expert_ids, route_weights, gate_weight, up_weight, down_weight):
    tokens, width = hidden_states.shape
    units = gate_weight.shape[2]
    n = n_node * n_local
    group = TILE if n % TILE == 0 else n
    strip, chunks = plan(width)
    nc = len(chunks)
    rows = n_local * TILE
    unf = unfold_matrix(group)
    vmem = pl.BlockSpec(memory_space=pltpu.VMEM)
    hbm = pl.BlockSpec(memory_space=pl.ANY)
    eo, mix = pl.pallas_call(
        functools.partial(expert_kernel, n_node, n_local, group, strip, chunks),
        out_shape=[
            jax.ShapeDtypeStruct((rows, strip), BF16),
            jax.ShapeDtypeStruct((FOLD, tokens, 3 * rows), BF16),
        ],
        in_specs=[hbm, vmem, vmem, vmem, vmem, hbm, hbm, hbm],
        out_specs=[vmem, vmem],
        scratch_shapes=[
            pltpu.VMEM((tokens, width), BF16),
            pltpu.VMEM((width, units), BF16),
            pltpu.VMEM((width, units), BF16),
            pltpu.VMEM((units, width), BF16),
            *[pltpu.VMEM((n_local, TILE, w), BF16) for _, w in chunks],
            *[pltpu.VMEM((n, TILE, w), BF16) for _ in range(2) for _, w in chunks],
            *[pltpu.VMEM((n + n_local, TILE, w), BF16) for _, w in chunks],
            *[pltpu.VMEM((n_local, TILE, w), BF16) for _, w in chunks],
            pltpu.SemaphoreType.DMA((nc, FOLD)),
            pltpu.SemaphoreType.DMA((3,)),
            pltpu.SemaphoreType.DMA((nc,)),
            pltpu.SemaphoreType.DMA((nc,)),
            pltpu.SemaphoreType.DMA((nc, n_node, 2)),
            pltpu.SemaphoreType.DMA((nc, n_node)),
            pltpu.SemaphoreType.DMA((nc, n_node)),
            pltpu.SemaphoreType.DMA((nc, n_node + 1)),
            pltpu.SemaphoreType.DMA((nc,)),
            pltpu.SemaphoreType.DMA((nc,)),
        ],
        compiler_params=pltpu.CompilerParams(
            collective_id=0, has_side_effects=True, vmem_limit_bytes=60 * 1024 * 1024
        ),
    )(
        hidden_states,
        expert_ids.T,
        route_weights.T,
        jnp.asarray(unf, BF16),
        jnp.asarray(unf.T, BF16),
        gate_weight,
        up_weight,
        down_weight,
    )
    return pl.pallas_call(
        functools.partial(combine_kernel, strip, chunks),
        out_shape=jax.ShapeDtypeStruct((tokens, width), BF16),
        in_specs=[hbm, hbm],
        out_specs=hbm,
        scratch_shapes=[
            pltpu.VMEM((rows, strip), BF16),
            pltpu.VMEM((FOLD, tokens, 3 * rows), BF16),
            pltpu.VMEM((tokens, width), BF16),
            pltpu.SemaphoreType.DMA((2,)),
            pltpu.SemaphoreType.DMA((nc, FOLD)),
        ],
        compiler_params=pltpu.CompilerParams(vmem_limit_bytes=60 * 1024 * 1024),
    )(eo, mix)


def solution(mesh):
    placed = (
        P(("parts", "node", "local"), None),
        P(("parts", "node", "local"), None),
        P(("parts", "node", "local"), None),
        P("local", None, "node"),
        P("local", None, "node"),
        P("local", "node", None),
    )
    return jax.shard_map(
        functools.partial(on_device, mesh.shape["node"], mesh.shape["local"]),
        mesh=mesh,
        in_specs=placed,
        out_specs=P(("parts", "node", "local"), None),
        check_vma=False,
    )
```

```python
import functools

import jax
import jax.numpy as jnp
import numpy as np
from jax import lax
from jax.experimental import pallas as pl
from jax.experimental.pallas import tpu as pltpu
from jax.sharding import PartitionSpec as P

EXPERTS = 256
CAP = 5
TILE = 16
FOLD = TILE // CAP
LANE = 128
PARTS = 4
F32 = jnp.float32
BF16 = jnp.bfloat16
MESH = pl.DeviceIdType.MESH


def plan(width):
    tiles = -(-width // (LANE * FOLD))
    base, extra = divmod(tiles, PARTS)
    chunks, off = [], 0
    for c in range(PARTS):
        w = (base + (c < extra)) * LANE
        chunks.append((off, w))
        off += w
    return tiles * LANE, chunks


def piece(width, strip, chunk, k):
    off, w = chunk
    start = k * strip + off
    return start, min(w, width - start)


def unfold_matrix(group):
    m = np.zeros((FOLD * group * CAP, group * TILE), np.float32)
    for k in range(FOLD):
        for s in range(group):
            for i in range(CAP):
                m[k * group * CAP + s * CAP + i, s * TILE + k * CAP + i] = 1
    return m


def expert_kernel(n_node, n_local, group, strip, chunks, hid, ids, rw, unf, fld, gate, up, down, eo, mix, *scratch):
    nc = len(chunks)
    hid_v, gate_v, up_v, down_v = scratch[:4]
    send_a = scratch[4:4 + nc]
    recv_a = scratch[4 + nc:4 + 2 * nc]
    send_b = scratch[4 + 2 * nc:4 + 3 * nc]
    recv_b = scratch[4 + 3 * nc:4 + 4 * nc]
    back = scratch[4 + 4 * nc:4 + 5 * nc]
    (hid_sem, wt_sem, loc_send, loc_recv, in_send, in_recv, out_send, out_recv, back_send, back_recv) = scratch[4 + 5 * nc:]
    n = n_node * n_local
    node, local = lax.axis_index("node"), lax.axis_index("local")
    tokens, width = hid.shape
    rows = n_local * TILE
    has_left, has_right = node > 0, node < n_node - 1
    is_first, is_last = node == 0, node == n_node - 1
    left, right = {"node": node - 1}, {"node": node + 1}

    def plane(ref, s):
        return ref.at[pl.ds(s * n_local, n_local)]

    def greet(where):
        pl.semaphore_signal(barrier, inc=1, device_id=where, device_id_type=MESH)

    barrier = pltpu.get_barrier_semaphore()

    @pl.loop(1, n_local)
    def _(d):
        greet({"local": lax.rem(local + d, n_local)})

    @pl.when(has_left)
    def _():
        greet(left)

    @pl.when(has_right)
    def _():
        greet(right)

    hid_copies = []
    for c in range(nc):
        for k in range(FOLD):
            start, w = piece(width, strip, chunks[c], k)
            copy = pltpu.make_async_copy(hid.at[:, pl.ds(start, w)], hid_v.at[:, pl.ds(start, w)], hid_sem.at[c, k])
            copy.start()
            hid_copies.append(copy)
    wt_copies = [
        pltpu.make_async_copy(src.at[0], dst, wt_sem.at[j])
        for j, (src, dst) in enumerate(((gate, gate_v), (up, up_v), (down, down_v)))
    ]

    row = lax.broadcasted_iota(jnp.int32, (rows, tokens), 0)
    want = (row >> 4) * (EXPERTS // n_local)
    low = row & (TILE - 1)
    strip_of = jnp.zeros_like(low)
    for k in range(1, FOLD + 1):
        strip_of += (low >= k * CAP).astype(jnp.int32)
    slot = low - strip_of * CAP
    match = jnp.zeros((rows, tokens), F32)
    share = jnp.zeros((rows, tokens), F32)
    for j in range(ids.shape[0]):
        hit = ids[j:j + 1, :] == want
        match += jnp.where(hit, 1.0, 0.0)
        share += jnp.where(hit, rw[j:j + 1, :], 0.0)
    before = lax.broadcasted_iota(jnp.int32, (tokens, tokens), 0) < lax.broadcasted_iota(jnp.int32, (tokens, tokens), 1)
    position = jnp.dot(match.astype(BF16), before.astype(F32).astype(BF16), preferred_element_type=F32)
    selected = (match > 0.0) & (position == slot.astype(F32))
    sel = [jnp.where(selected & (strip_of == k), 1.0, 0.0).astype(BF16) for k in range(FOLD)]

    def to_locals(src, base, dst, index, s_sem, r_sem):
        @pl.loop(1, n_local)
        def _(d):
            peer = lax.rem(local + d, n_local)
            pltpu.make_async_remote_copy(
                src_ref=src.at[base + peer],
                dst_ref=dst.at[index],
                send_sem=s_sem,
                recv_sem=r_sem,
                device_id={"local": peer},
                device_id_type=MESH,
            ).start()

    def drain_locals(ref, sem):
        others = ref.at[pl.ds(0, n_local - 1)]
        pltpu.make_async_copy(others, others, sem).wait()

    def in_copy(c, s, where, way):
        return pltpu.make_async_remote_copy(
            src_ref=plane(recv_a[c], s),
            dst_ref=plane(recv_a[c], s),
            send_sem=in_send.at[c, s, way],
            recv_sem=in_recv.at[c, s],
            device_id=where,
            device_id_type=MESH,
        )

    def out_copy(c, s, place, where):
        return pltpu.make_async_remote_copy(
            src_ref=plane(send_b[c], s),
            dst_ref=plane(recv_b[c], place),
            send_sem=out_send.at[c, s],
            recv_sem=out_recv.at[c, place],
            device_id=where,
            device_id_type=MESH,
        )

    def arrived(ref, sem):
        pltpu.make_async_copy(ref, ref, sem).wait()

    for c in range(nc):
        w_full = chunks[c][1]
        total = None
        for k in range(FOLD):
            hid_copies[c * FOLD + k].wait()
            start, w = piece(width, strip, chunks[c], k)
            part = jnp.dot(sel[k], hid_v[:, start:start + w], preferred_element_type=F32)
            if w < w_full:
                part = jnp.concatenate([part, jnp.zeros((rows, w_full - w), F32)], axis=1)
            total = part if total is None else total + part
        send_a[c][...] = total.astype(BF16).reshape(n_local, TILE, w_full)
        if c == 0:
            pl.semaphore_wait(barrier, n_local - 1 + has_left.astype(jnp.int32) + has_right.astype(jnp.int32))
        to_locals(send_a[c], 0, recv_a[c], node * n_local + local, loc_send.at[c], loc_recv.at[c])
        recv_a[c][node * n_local + local] = send_a[c][local]

    for c in range(nc):
        drain_locals(send_a[c], loc_recv.at[c])

        @pl.when(has_right)
        def _():
            in_copy(c, node, right, 0).start()

        @pl.when(has_left)
        def _():
            in_copy(c, node, left, 1).start()

    for copy in wt_copies:
        copy.start()

    mixed = jnp.where(selected, share, 0.0)
    for k in range(FOLD):
        m = jnp.where(strip_of == k, mixed, 0.0)
        hi = m.astype(BF16).astype(F32)
        mid = (m - hi).astype(BF16).astype(F32)
        lo = m - hi - mid
        mix[k] = jnp.concatenate([hi, mid, lo], axis=0).T.astype(BF16)

    for c in range(nc):
        @pl.when(is_first)
        def _():
            recv_b[c][0:n_local] = jnp.zeros((n_local, TILE, chunks[c][1]), BF16)

        @pl.when(is_last)
        def _():
            recv_b[c][n:n + n_local] = jnp.zeros((n_local, TILE, chunks[c][1]), BF16)

    half_planes = n_node // 2
    half = half_planes * n_local
    near_plane = lax.select(node < half_planes, 0, half_planes)
    far_plane = half_planes - near_plane
    unfold, fold = unf[...], fld[...]
    per = group * CAP

    def pass_on(c, h):
        @pl.when((node - h >= 0) & has_right)
        def _():
            arrived(plane(recv_a[c], node - h), in_recv.at[c, node - h])
            in_copy(c, node - h, right, 0).start()

        @pl.when((node + h < n_node) & has_left)
        def _():
            arrived(plane(recv_a[c], node + h), in_recv.at[c, node + h])
            in_copy(c, node + h, left, 1).start()

    def await_planes(c, first, last):
        @pl.when(is_first)
        def _():
            @pl.loop(*first)
            def _(s):
                arrived(plane(recv_a[c], s), in_recv.at[c, s])

        @pl.when(is_last)
        def _():
            @pl.loop(*last)
            def _(s):
                arrived(plane(recv_a[c], s), in_recv.at[c, s])

    def project(c, base, sums):
        w_full = chunks[c][1]
        flat = [
            jnp.dot(
                unfold,
                recv_a[c][pl.ds(base + g, group)].reshape(group * TILE, w_full),
                preferred_element_type=F32,
            )
            for g in range(0, half, group)
        ]
        for k in range(FOLD):
            start, w = piece(width, strip, chunks[c], k)
            x = [f[k * per:(k + 1) * per, :w] for f in flat]
            x = (x[0] if len(x) == 1 else jnp.concatenate(x, axis=0)).astype(BF16)
            g = jnp.dot(x, gate_v[start:start + w, :], preferred_element_type=F32)
            u = jnp.dot(x, up_v[start:start + w, :], preferred_element_type=F32)
            sums = (g, u) if sums is None else (sums[0] + g, sums[1] + u)
        return sums

    def activate(sums):
        return (sums[0] / (1.0 + jnp.exp(-sums[0])) * sums[1]).astype(BF16)

    def partial_sums(c, base, act):
        w_full = chunks[c][1]
        y = []
        for k in range(FOLD):
            start, w = piece(width, strip, chunks[c], k)
            part = jnp.dot(act, down_v[:, start:start + w], preferred_element_type=F32)
            if w < w_full:
                part = jnp.concatenate([part, jnp.zeros((part.shape[0], w_full - w), F32)], axis=1)
            y.append(part)
        for j, g in enumerate(range(0, half, group)):
            stack = jnp.concatenate([p[j * per:(j + 1) * per] for p in y], axis=0).astype(BF16)
            folded = jnp.dot(fold, stack, preferred_element_type=F32).astype(BF16)
            send_b[c][pl.ds(base + g, group)] = folded.reshape(group, TILE, w_full)

    @pl.loop(1, half_planes)
    def _(h):
        for c in range(nc):
            pass_on(c, h)

    sums = None
    for c in range(nc):
        await_planes(c, (1, half_planes), (half_planes, n_node - 1))
        if c == 0:
            wt_copies[0].wait()
            wt_copies[1].wait()
        sums = project(c, near_plane * n_local, sums)

        @pl.loop(half_planes, n_node)
        def _(h):
            pass_on(c, h)

    act = activate(sums)
    wt_copies[2].wait()
    for c in range(nc):
        partial_sums(c, near_plane * n_local, act)

        @pl.when(is_first)
        def _():
            @pl.loop(1, half_planes)
            def _(e):
                s = half_planes - e
                out_copy(c, s, s, right).start()

        @pl.when(is_last)
        def _():
            @pl.loop(half_planes, n_node - 1)
            def _(s):
                out_copy(c, s, lax.select(node - s == 1, n_node, s), left).start()

    sums = None
    for c in range(nc):
        await_planes(c, (half_planes, n_node), (0, half_planes))
        sums = project(c, far_plane * n_local, sums)
    act = activate(sums)

    def add(c, s):
        there = pl.ds(s * n_local, n_local)
        send_b[c][there] = (send_b[c][there].astype(F32) + recv_b[c][there].astype(F32)).astype(BF16)

    for c in range(nc):
        partial_sums(c, far_plane * n_local, act)

        @pl.when(is_first)
        def _():
            out_copy(c, n_node - 1, n_node - 1, right).start()

        @pl.when(is_last)
        def _():
            out_copy(c, 0, lax.select(node == 1, n_node, 0), left).start()

    @pl.loop(0, n_node - 1)
    def _(e):
        h = n_node - 1 - e
        for c in range(nc):
            @pl.when((node + h < n_node) & (h < n_node - 1) & (has_left | (h >= half_planes)))
            def _():
                @pl.when(has_left)
                def _():
                    arrived(plane(recv_b[c], node + h), out_recv.at[c, node + h])
                    add(c, node + h)

                out_copy(c, node + h, node + h, right).start()

            @pl.when((node - h >= 0) & (h < n_node - 1) & (has_right | (h >= half_planes)))
            def _():
                @pl.when(has_right)
                def _():
                    arrived(plane(recv_b[c], node - h), out_recv.at[c, node - h])
                    add(c, node - h)

                out_copy(c, node - h, lax.select(h == 1, n_node, node - h), left).start()

    for c in range(nc):
        @pl.when(has_left)
        def _():
            arrived(plane(recv_b[c], node), out_recv.at[c, node])

        @pl.when(has_right)
        def _():
            arrived(plane(recv_b[c], n_node), out_recv.at[c, n_node])

        here = pl.ds(node * n_local, n_local)
        total = send_b[c][here].astype(F32) + recv_b[c][here].astype(F32) + recv_b[c][n:n + n_local].astype(F32)
        send_b[c][here] = total.astype(BF16)
        to_locals(send_b[c], node * n_local, back[c], local, back_send.at[c], back_recv.at[c])
        back[c][local] = send_b[c][node * n_local + local]

    for c in range(nc):
        off, w_full = chunks[c]
        drain_locals(send_a[c], back_recv.at[c])
        eo[:, off:off + w_full] = back[c][...].reshape(rows, w_full)

    for c in range(nc):
        drain_locals(send_a[c], loc_send.at[c])
        drain_locals(send_a[c], back_send.at[c])

        @pl.loop(0, n_node)
        def _(s):
            @pl.when((s <= node) & has_right)
            def _():
                arrived(plane(recv_a[c], s), in_send.at[c, s, 0])

            @pl.when((s >= node) & has_left)
            def _():
                arrived(plane(recv_a[c], s), in_send.at[c, s, 1])

            @pl.when(s != node)
            def _():
                arrived(plane(send_b[c], s), out_send.at[c, s])


def combine_kernel(strip, chunks, eo_hbm, mix_hbm, out, eo, mix, buf, in_sems, sems):
    width = out.shape[1]
    loads = [
        pltpu.make_async_copy(src, dst, in_sems.at[j])
        for j, (src, dst) in enumerate(((eo_hbm, eo), (mix_hbm, mix)))
    ]
    for copy in loads:
        copy.start()
    for copy in loads:
        copy.wait()
    copies = []
    for c, (off, w_full) in enumerate(chunks):
        block = eo[:, off:off + w_full]
        block = jnp.concatenate([block, block, block], axis=0)
        for k in range(FOLD):
            start, w = piece(width, strip, chunks[c], k)
            buf[:, start:start + w] = jnp.dot(mix[k], block[:, :w], preferred_element_type=F32).astype(BF16)
            copy = pltpu.make_async_copy(buf.at[:, pl.ds(start, w)], out.at[:, pl.ds(start, w)], sems.at[c, k])
            copy.start()
            copies.append(copy)
    for copy in copies:
        copy.wait()


def on_device(n_node, n_local, hidden_states, expert_ids, route_weights, gate_weight, up_weight, down_weight):
    tokens, width = hidden_states.shape
    units = gate_weight.shape[2]
    n = n_node * n_local
    half = n // 2
    group = TILE if half % TILE == 0 else half
    strip, chunks = plan(width)
    nc = len(chunks)
    rows = n_local * TILE
    unf = unfold_matrix(group)
    vmem = pl.BlockSpec(memory_space=pltpu.VMEM)
    hbm = pl.BlockSpec(memory_space=pl.ANY)
    eo, mix = pl.pallas_call(
        functools.partial(expert_kernel, n_node, n_local, group, strip, chunks),
        out_shape=[
            jax.ShapeDtypeStruct((rows, strip), BF16),
            jax.ShapeDtypeStruct((FOLD, tokens, 3 * rows), BF16),
        ],
        in_specs=[hbm, vmem, vmem, vmem, vmem, hbm, hbm, hbm],
        out_specs=[vmem, vmem],
        scratch_shapes=[
            pltpu.VMEM((tokens, width), BF16),
            pltpu.VMEM((width, units), BF16),
            pltpu.VMEM((width, units), BF16),
            pltpu.VMEM((units, width), BF16),
            *[pltpu.VMEM((n_local, TILE, w), BF16) for _, w in chunks],
            *[pltpu.VMEM((n, TILE, w), BF16) for _ in range(2) for _, w in chunks],
            *[pltpu.VMEM((n + n_local, TILE, w), BF16) for _, w in chunks],
            *[pltpu.VMEM((n_local, TILE, w), BF16) for _, w in chunks],
            pltpu.SemaphoreType.DMA((nc, FOLD)),
            pltpu.SemaphoreType.DMA((3,)),
            pltpu.SemaphoreType.DMA((nc,)),
            pltpu.SemaphoreType.DMA((nc,)),
            pltpu.SemaphoreType.DMA((nc, n_node, 2)),
            pltpu.SemaphoreType.DMA((nc, n_node)),
            pltpu.SemaphoreType.DMA((nc, n_node)),
            pltpu.SemaphoreType.DMA((nc, n_node + 1)),
            pltpu.SemaphoreType.DMA((nc,)),
            pltpu.SemaphoreType.DMA((nc,)),
        ],
        compiler_params=pltpu.CompilerParams(
            collective_id=0, has_side_effects=True, vmem_limit_bytes=60 * 1024 * 1024
        ),
    )(
        hidden_states,
        expert_ids.T,
        route_weights.T,
        jnp.asarray(unf, BF16),
        jnp.asarray(unf.T, BF16),
        gate_weight,
        up_weight,
        down_weight,
    )
    return pl.pallas_call(
        functools.partial(combine_kernel, strip, chunks),
        out_shape=jax.ShapeDtypeStruct((tokens, width), BF16),
        in_specs=[hbm, hbm],
        out_specs=hbm,
        scratch_shapes=[
            pltpu.VMEM((rows, strip), BF16),
            pltpu.VMEM((FOLD, tokens, 3 * rows), BF16),
            pltpu.VMEM((tokens, width), BF16),
            pltpu.SemaphoreType.DMA((2,)),
            pltpu.SemaphoreType.DMA((nc, FOLD)),
        ],
        compiler_params=pltpu.CompilerParams(vmem_limit_bytes=60 * 1024 * 1024),
    )(eo, mix)


def solution(mesh):
    placed = (
        P(("parts", "node", "local"), None),
        P(("parts", "node", "local"), None),
        P(("parts", "node", "local"), None),
        P("local", None, "node"),
        P("local", None, "node"),
        P("local", "node", None),
    )
    return jax.shard_map(
        functools.partial(on_device, mesh.shape["node"], mesh.shape["local"]),
        mesh=mesh,
        in_specs=placed,
        out_specs=P(("parts", "node", "local"), None),
        check_vma=False,
    )
```

```python
import functools

import jax
import jax.numpy as jnp
import numpy as np
from jax import lax
from jax.experimental import pallas as pl
from jax.experimental.pallas import tpu as pltpu
from jax.sharding import PartitionSpec as P

EXPERTS = 256
CAP = 5
TILE = 16
FOLD = TILE // CAP
LANE = 128
PARTS = 6
F32 = jnp.float32
BF16 = jnp.bfloat16
MESH = pl.DeviceIdType.MESH


def plan(width):
    tiles = -(-width // (LANE * FOLD))
    base, extra = divmod(tiles, PARTS)
    chunks, off = [], 0
    for c in range(PARTS):
        w = (base + (c < extra)) * LANE
        chunks.append((off, w))
        off += w
    return tiles * LANE, chunks


def piece(width, strip, chunk, k):
    off, w = chunk
    start = k * strip + off
    return start, min(w, width - start)


def unfold_matrix(group):
    m = np.zeros((FOLD * group * CAP, group * TILE), np.float32)
    for k in range(FOLD):
        for s in range(group):
            for i in range(CAP):
                m[k * group * CAP + s * CAP + i, s * TILE + k * CAP + i] = 1
    return m


def expert_kernel(n_node, n_local, group, strip, chunks, hid, ids, rw, unf, fld, gate, up, down, eo, mix, *scratch):
    nc = len(chunks)
    hid_v, gate_v, up_v, down_v = scratch[:4]
    send_a = scratch[4:4 + nc]
    recv_a = scratch[4 + nc:4 + 2 * nc]
    send_b = scratch[4 + 2 * nc:4 + 3 * nc]
    recv_b = scratch[4 + 3 * nc:4 + 4 * nc]
    back = scratch[4 + 4 * nc:4 + 5 * nc]
    (hid_sem, wt_sem, loc_send, loc_recv, in_send, in_recv, out_send, out_recv, back_send, back_recv) = scratch[4 + 5 * nc:]
    n = n_node * n_local
    node, local = lax.axis_index("node"), lax.axis_index("local")
    tokens, width = hid.shape
    rows = n_local * TILE
    has_left, has_right = node > 0, node < n_node - 1
    is_first, is_last = node == 0, node == n_node - 1
    left, right = {"node": node - 1}, {"node": node + 1}

    def plane(ref, s):
        return ref.at[pl.ds(s * n_local, n_local)]

    def greet(where):
        pl.semaphore_signal(barrier, inc=1, device_id=where, device_id_type=MESH)

    barrier = pltpu.get_barrier_semaphore()

    @pl.loop(1, n_local)
    def _(d):
        greet({"local": lax.rem(local + d, n_local)})

    @pl.when(has_left)
    def _():
        greet(left)

    @pl.when(has_right)
    def _():
        greet(right)

    hid_copies = []
    for c in range(nc):
        for k in range(FOLD):
            start, w = piece(width, strip, chunks[c], k)
            copy = pltpu.make_async_copy(hid.at[:, pl.ds(start, w)], hid_v.at[:, pl.ds(start, w)], hid_sem.at[c, k])
            copy.start()
            hid_copies.append(copy)
    wt_copies = [
        pltpu.make_async_copy(src.at[0], dst, wt_sem.at[j])
        for j, (src, dst) in enumerate(((gate, gate_v), (up, up_v), (down, down_v)))
    ]

    row = lax.broadcasted_iota(jnp.int32, (rows, tokens), 0)
    want = (row >> 4) * (EXPERTS // n_local)
    low = row & (TILE - 1)
    strip_of = jnp.zeros_like(low)
    for k in range(1, FOLD + 1):
        strip_of += (low >= k * CAP).astype(jnp.int32)
    slot = low - strip_of * CAP
    match = jnp.zeros((rows, tokens), F32)
    share = jnp.zeros((rows, tokens), F32)
    for j in range(ids.shape[0]):
        hit = ids[j:j + 1, :] == want
        match += jnp.where(hit, 1.0, 0.0)
        share += jnp.where(hit, rw[j:j + 1, :], 0.0)
    before = lax.broadcasted_iota(jnp.int32, (tokens, tokens), 0) < lax.broadcasted_iota(jnp.int32, (tokens, tokens), 1)
    position = jnp.dot(match.astype(BF16), before.astype(F32).astype(BF16), preferred_element_type=F32)
    selected = (match > 0.0) & (position == slot.astype(F32))
    sel = [jnp.where(selected & (strip_of == k), 1.0, 0.0).astype(BF16) for k in range(FOLD)]

    def to_locals(src, base, dst, index, s_sem, r_sem):
        @pl.loop(1, n_local)
        def _(d):
            peer = lax.rem(local + d, n_local)
            pltpu.make_async_remote_copy(
                src_ref=src.at[base + peer],
                dst_ref=dst.at[index],
                send_sem=s_sem,
                recv_sem=r_sem,
                device_id={"local": peer},
                device_id_type=MESH,
            ).start()

    def drain_locals(ref, sem):
        others = ref.at[pl.ds(0, n_local - 1)]
        pltpu.make_async_copy(others, others, sem).wait()

    def in_copy(c, s, where, way):
        return pltpu.make_async_remote_copy(
            src_ref=plane(recv_a[c], s),
            dst_ref=plane(recv_a[c], s),
            send_sem=in_send.at[c, s, way],
            recv_sem=in_recv.at[c, s],
            device_id=where,
            device_id_type=MESH,
        )

    def out_copy(c, s, place, where):
        return pltpu.make_async_remote_copy(
            src_ref=plane(send_b[c], s),
            dst_ref=plane(recv_b[c], place),
            send_sem=out_send.at[c, s],
            recv_sem=out_recv.at[c, place],
            device_id=where,
            device_id_type=MESH,
        )

    def arrived(ref, sem):
        pltpu.make_async_copy(ref, ref, sem).wait()

    for c in range(nc):
        w_full = chunks[c][1]
        total = None
        for k in range(FOLD):
            hid_copies[c * FOLD + k].wait()
            start, w = piece(width, strip, chunks[c], k)
            part = jnp.dot(sel[k], hid_v[:, start:start + w], preferred_element_type=F32)
            if w < w_full:
                part = jnp.concatenate([part, jnp.zeros((rows, w_full - w), F32)], axis=1)
            total = part if total is None else total + part
        send_a[c][...] = total.astype(BF16).reshape(n_local, TILE, w_full)
        if c == 0:
            pl.semaphore_wait(barrier, n_local - 1 + has_left.astype(jnp.int32) + has_right.astype(jnp.int32))
        to_locals(send_a[c], 0, recv_a[c], node * n_local + local, loc_send.at[c], loc_recv.at[c])
        recv_a[c][node * n_local + local] = send_a[c][local]

    for c in range(nc):
        drain_locals(send_a[c], loc_recv.at[c])

        @pl.when(has_right)
        def _():
            in_copy(c, node, right, 0).start()

        @pl.when(has_left)
        def _():
            in_copy(c, node, left, 1).start()

    for copy in wt_copies:
        copy.start()

    mixed = jnp.where(selected, share, 0.0)
    for k in range(FOLD):
        m = jnp.where(strip_of == k, mixed, 0.0)
        hi = m.astype(BF16).astype(F32)
        mid = (m - hi).astype(BF16).astype(F32)
        lo = m - hi - mid
        mix[k] = jnp.concatenate([hi, mid, lo], axis=0).T.astype(BF16)

    for c in range(nc):
        @pl.when(is_first)
        def _():
            recv_b[c][0:n_local] = jnp.zeros((n_local, TILE, chunks[c][1]), BF16)

        @pl.when(is_last)
        def _():
            recv_b[c][n:n + n_local] = jnp.zeros((n_local, TILE, chunks[c][1]), BF16)

    half_planes = n_node // 2
    half = half_planes * n_local
    near_plane = lax.select(node < half_planes, 0, half_planes)
    far_plane = half_planes - near_plane
    unfold, fold = unf[...], fld[...]
    per = group * CAP

    def pass_on(c, h):
        @pl.when((node - h >= 0) & has_right)
        def _():
            arrived(plane(recv_a[c], node - h), in_recv.at[c, node - h])
            in_copy(c, node - h, right, 0).start()

        @pl.when((node + h < n_node) & has_left)
        def _():
            arrived(plane(recv_a[c], node + h), in_recv.at[c, node + h])
            in_copy(c, node + h, left, 1).start()

    def await_planes(c, first, last):
        @pl.when(is_first)
        def _():
            @pl.loop(*first)
            def _(s):
                arrived(plane(recv_a[c], s), in_recv.at[c, s])

        @pl.when(is_last)
        def _():
            @pl.loop(*last)
            def _(s):
                arrived(plane(recv_a[c], s), in_recv.at[c, s])

    def project(c, base, sums):
        w_full = chunks[c][1]
        flat = [
            jnp.dot(
                unfold,
                recv_a[c][pl.ds(base + g, group)].reshape(group * TILE, w_full),
                preferred_element_type=F32,
            )
            for g in range(0, half, group)
        ]
        for k in range(FOLD):
            start, w = piece(width, strip, chunks[c], k)
            x = [f[k * per:(k + 1) * per, :w] for f in flat]
            x = (x[0] if len(x) == 1 else jnp.concatenate(x, axis=0)).astype(BF16)
            g = jnp.dot(x, gate_v[start:start + w, :], preferred_element_type=F32)
            u = jnp.dot(x, up_v[start:start + w, :], preferred_element_type=F32)
            sums = (g, u) if sums is None else (sums[0] + g, sums[1] + u)
        return sums

    def activate(sums):
        return (sums[0] / (1.0 + jnp.exp(-sums[0])) * sums[1]).astype(BF16)

    def partial_sums(c, base, act):
        w_full = chunks[c][1]
        y = []
        for k in range(FOLD):
            start, w = piece(width, strip, chunks[c], k)
            part = jnp.dot(act, down_v[:, start:start + w], preferred_element_type=F32)
            if w < w_full:
                part = jnp.concatenate([part, jnp.zeros((part.shape[0], w_full - w), F32)], axis=1)
            y.append(part)
        for j, g in enumerate(range(0, half, group)):
            stack = jnp.concatenate([p[j * per:(j + 1) * per] for p in y], axis=0).astype(BF16)
            folded = jnp.dot(fold, stack, preferred_element_type=F32).astype(BF16)
            send_b[c][pl.ds(base + g, group)] = folded.reshape(group, TILE, w_full)

    @pl.loop(1, half_planes)
    def _(h):
        for c in range(nc):
            pass_on(c, h)

    sums = None
    for c in range(nc):
        await_planes(c, (1, half_planes), (half_planes, n_node - 1))
        if c == 0:
            wt_copies[0].wait()
            wt_copies[1].wait()
        sums = project(c, near_plane * n_local, sums)

        @pl.loop(half_planes, n_node)
        def _(h):
            pass_on(c, h)

    act = activate(sums)
    wt_copies[2].wait()
    for c in range(nc):
        partial_sums(c, near_plane * n_local, act)

        @pl.when(is_first)
        def _():
            @pl.loop(1, half_planes)
            def _(e):
                s = half_planes - e
                out_copy(c, s, s, right).start()

        @pl.when(is_last)
        def _():
            @pl.loop(half_planes, n_node - 1)
            def _(s):
                out_copy(c, s, lax.select(node - s == 1, n_node, s), left).start()

    sums = None
    for c in range(nc):
        await_planes(c, (half_planes, n_node), (0, half_planes))
        sums = project(c, far_plane * n_local, sums)
    act = activate(sums)

    def add(c, s):
        there = pl.ds(s * n_local, n_local)
        send_b[c][there] = (send_b[c][there].astype(F32) + recv_b[c][there].astype(F32)).astype(BF16)

    for c in range(nc):
        partial_sums(c, far_plane * n_local, act)

        @pl.when(is_first)
        def _():
            out_copy(c, n_node - 1, n_node - 1, right).start()

        @pl.when(is_last)
        def _():
            out_copy(c, 0, lax.select(node == 1, n_node, 0), left).start()

    @pl.loop(0, n_node - 1)
    def _(e):
        h = n_node - 1 - e
        for c in range(nc):
            @pl.when((node + h < n_node) & (h < n_node - 1) & (has_left | (h >= half_planes)))
            def _():
                @pl.when(has_left)
                def _():
                    arrived(plane(recv_b[c], node + h), out_recv.at[c, node + h])
                    add(c, node + h)

                out_copy(c, node + h, node + h, right).start()

            @pl.when((node - h >= 0) & (h < n_node - 1) & (has_right | (h >= half_planes)))
            def _():
                @pl.when(has_right)
                def _():
                    arrived(plane(recv_b[c], node - h), out_recv.at[c, node - h])
                    add(c, node - h)

                out_copy(c, node - h, lax.select(h == 1, n_node, node - h), left).start()

    for c in range(nc):
        @pl.when(has_left)
        def _():
            arrived(plane(recv_b[c], node), out_recv.at[c, node])

        @pl.when(has_right)
        def _():
            arrived(plane(recv_b[c], n_node), out_recv.at[c, n_node])

        here = pl.ds(node * n_local, n_local)
        total = send_b[c][here].astype(F32) + recv_b[c][here].astype(F32) + recv_b[c][n:n + n_local].astype(F32)
        send_b[c][here] = total.astype(BF16)
        to_locals(send_b[c], node * n_local, back[c], local, back_send.at[c], back_recv.at[c])
        back[c][local] = send_b[c][node * n_local + local]

    for c in range(nc):
        off, w_full = chunks[c]
        drain_locals(send_a[c], back_recv.at[c])
        eo[:, off:off + w_full] = back[c][...].reshape(rows, w_full)

    for c in range(nc):
        drain_locals(send_a[c], loc_send.at[c])
        drain_locals(send_a[c], back_send.at[c])

        @pl.loop(0, n_node)
        def _(s):
            @pl.when((s <= node) & has_right)
            def _():
                arrived(plane(recv_a[c], s), in_send.at[c, s, 0])

            @pl.when((s >= node) & has_left)
            def _():
                arrived(plane(recv_a[c], s), in_send.at[c, s, 1])

            @pl.when(s != node)
            def _():
                arrived(plane(send_b[c], s), out_send.at[c, s])


def combine_kernel(strip, chunks, eo_hbm, mix_hbm, out, eo, mix, buf, in_sems, sems):
    width = out.shape[1]
    loads = [
        pltpu.make_async_copy(src, dst, in_sems.at[j])
        for j, (src, dst) in enumerate(((eo_hbm, eo), (mix_hbm, mix)))
    ]
    for copy in loads:
        copy.start()
    for copy in loads:
        copy.wait()
    copies = []
    for c, (off, w_full) in enumerate(chunks):
        block = eo[:, off:off + w_full]
        block = jnp.concatenate([block, block, block], axis=0)
        for k in range(FOLD):
            start, w = piece(width, strip, chunks[c], k)
            buf[:, start:start + w] = jnp.dot(mix[k], block[:, :w], preferred_element_type=F32).astype(BF16)
            copy = pltpu.make_async_copy(buf.at[:, pl.ds(start, w)], out.at[:, pl.ds(start, w)], sems.at[c, k])
            copy.start()
            copies.append(copy)
    for copy in copies:
        copy.wait()


def on_device(n_node, n_local, hidden_states, expert_ids, route_weights, gate_weight, up_weight, down_weight):
    tokens, width = hidden_states.shape
    units = gate_weight.shape[2]
    n = n_node * n_local
    half = n // 2
    group = TILE if half % TILE == 0 else half
    strip, chunks = plan(width)
    nc = len(chunks)
    rows = n_local * TILE
    unf = unfold_matrix(group)
    vmem = pl.BlockSpec(memory_space=pltpu.VMEM)
    hbm = pl.BlockSpec(memory_space=pl.ANY)
    eo, mix = pl.pallas_call(
        functools.partial(expert_kernel, n_node, n_local, group, strip, chunks),
        out_shape=[
            jax.ShapeDtypeStruct((rows, strip), BF16),
            jax.ShapeDtypeStruct((FOLD, tokens, 3 * rows), BF16),
        ],
        in_specs=[hbm, vmem, vmem, vmem, vmem, hbm, hbm, hbm],
        out_specs=[vmem, vmem],
        scratch_shapes=[
            pltpu.VMEM((tokens, width), BF16),
            pltpu.VMEM((width, units), BF16),
            pltpu.VMEM((width, units), BF16),
            pltpu.VMEM((units, width), BF16),
            *[pltpu.VMEM((n_local, TILE, w), BF16) for _, w in chunks],
            *[pltpu.VMEM((n, TILE, w), BF16) for _ in range(2) for _, w in chunks],
            *[pltpu.VMEM((n + n_local, TILE, w), BF16) for _, w in chunks],
            *[pltpu.VMEM((n_local, TILE, w), BF16) for _, w in chunks],
            pltpu.SemaphoreType.DMA((nc, FOLD)),
            pltpu.SemaphoreType.DMA((3,)),
            pltpu.SemaphoreType.DMA((nc,)),
            pltpu.SemaphoreType.DMA((nc,)),
            pltpu.SemaphoreType.DMA((nc, n_node, 2)),
            pltpu.SemaphoreType.DMA((nc, n_node)),
            pltpu.SemaphoreType.DMA((nc, n_node)),
            pltpu.SemaphoreType.DMA((nc, n_node + 1)),
            pltpu.SemaphoreType.DMA((nc,)),
            pltpu.SemaphoreType.DMA((nc,)),
        ],
        compiler_params=pltpu.CompilerParams(
            collective_id=0, has_side_effects=True, vmem_limit_bytes=60 * 1024 * 1024
        ),
    )(
        hidden_states,
        expert_ids.T,
        route_weights.T,
        jnp.asarray(unf, BF16),
        jnp.asarray(unf.T, BF16),
        gate_weight,
        up_weight,
        down_weight,
    )
    return pl.pallas_call(
        functools.partial(combine_kernel, strip, chunks),
        out_shape=jax.ShapeDtypeStruct((tokens, width), BF16),
        in_specs=[hbm, hbm],
        out_specs=hbm,
        scratch_shapes=[
            pltpu.VMEM((rows, strip), BF16),
            pltpu.VMEM((FOLD, tokens, 3 * rows), BF16),
            pltpu.VMEM((tokens, width), BF16),
            pltpu.SemaphoreType.DMA((2,)),
            pltpu.SemaphoreType.DMA((nc, FOLD)),
        ],
        compiler_params=pltpu.CompilerParams(vmem_limit_bytes=60 * 1024 * 1024),
    )(eo, mix)


def solution(mesh):
    placed = (
        P(("parts", "node", "local"), None),
        P(("parts", "node", "local"), None),
        P(("parts", "node", "local"), None),
        P("local", None, "node"),
        P("local", None, "node"),
        P("local", "node", None),
    )
    return jax.shard_map(
        functools.partial(on_device, mesh.shape["node"], mesh.shape["local"]),
        mesh=mesh,
        in_specs=placed,
        out_specs=P(("parts", "node", "local"), None),
        check_vma=False,
    )
```
